32 devices in a mesh: axial: 8 (over z, x), cross: 4 (over y, core).
Axes of the slice: x: 2, y: 2, z: 4, core: 2. Of those that a mesh axis runs over, the one named last changes fastest.
Arguments:
- cotangent: float32 [128, 32, 16, 128], P('axial', None, 'cross'), may hold values from -8 to 8
- diag_blocks: float32 [128, 32, 32], P('axial'), as said below
- lower_rates: float32 [128, 32], P('axial'), as said below
- upper_rates: float32 [128, 32], P('axial'), as said below
- cross_rate: float32 [32], replicated, may hold values from 0.02 to 0.24
- bin_profile: float32 [32], replicated, may hold values from 0.1 to 1
- open_cells: int32 [16, 128], replicated, may hold values 0 or 1
- segment_ids: int32 [128, 16], P('axial', 'cross'), may hold values from 0 to 127
Outputs:
- grad_state: float32 [128, 32, 16, 128], P('axial', None, 'cross')
- grad_emission: float32 [128], P(('axial', 'cross'))
The draws below stay inside these ranges and needn't reach their ends.
Inputs may be any that keep to these rules, and one draw needn't show every extreme that they name: In every row (i, b) of the forward operator, diag_blocks[i, b, b] exceeds lower_rates[i, b] + upper_rates[i, b] + the sum of the magnitudes of the other entries of diag_blocks[i, b, :] by 1 or more. `lower_rates`: Positive. `upper_rates`: Positive.
All inputs are finite; a program needn't handle non-finite values.
Results may differ from the reference program's by a relative error of at most 0.0003.
Values sent between devices are 32-bit elements; how exact they have to be, the bound alone decides.
A program may use at most 64 MiB of HBM per device.

```python
import math
import jax
import jax.numpy as jnp
from jax import lax

B = 32
CA = 16
Y_DEV = 4
NZ = 128
AXIAL_CELLS = 128
NY = 16
SEGMENTS = 128
N_CROSS = 4


def spread(key, shape, low_end, high_end):
    return jnp.exp(jax.random.uniform(key, shape, jnp.float32, math.log(low_end), math.log(high_end)))


def operator_law(key):
    base_key = jax.random.fold_in(key, 41)
    random_key_list = jax.random.split(base_key, 10)
    slow_share = 0.5
    slow_low = 0.04
    slow_high = 0.25
    slow_bins = jax.random.uniform(random_key_list[0], (B,), jnp.float32) < slow_share
    square_span = float(8 * CA * (8 * CA))
    bin_rate = jnp.where(slow_bins, square_span * spread(random_key_list[1], (B,), slow_low, slow_high), spread(random_key_list[2], (B,), 0.3, 3.0))
    settled_dust = jnp.where(slow_bins, spread(random_key_list[3], (B,), 0.05, 0.5), spread(random_key_list[4], (B,), 0.5, 3.0))
    block_factor = jnp.repeat(spread(random_key_list[5], (AXIAL_CELLS // CA,), 0.6, 1.6), CA)
    cell_scale = bin_rate[None, :] * block_factor[:, None]
    lower_side_rates = cell_scale * jax.random.uniform(random_key_list[6], (AXIAL_CELLS, B), jnp.float32, 0.5, 1.5)
    upper_side_rates = cell_scale * jax.random.uniform(random_key_list[7], (AXIAL_CELLS, B), jnp.float32, 0.5, 1.5)
    spike_cells = (jax.random.uniform(random_key_list[8], (AXIAL_CELLS,), jnp.float32) < 4.0 / AXIAL_CELLS).astype(jnp.float32)
    safety_margin = (1.0 + settled_dust)[None, :] + spike_cells[:, None] * 0.5 * (lower_side_rates + upper_side_rates)
    off_diag = 1.0 - jnp.eye(B, dtype=jnp.float32)
    bin_coupling = jax.random.uniform(random_key_list[9], (AXIAL_CELLS, B, B), jnp.float32, -1.0, 1.0) * (0.5 / (B - 1)) * (1.0 + settled_dust)[None, :, None] * off_diag
    centre = safety_margin + 0.5 * (1.0 + settled_dust)[None, :] + lower_side_rates + upper_side_rates
    blocks = bin_coupling + centre[:, :, None] * jnp.eye(B, dtype=jnp.float32)[None, :, :]
    return (blocks, lower_side_rates, upper_side_rates)


def draw_diag_blocks(key, part):
    return operator_law(key)[0]


def draw_lower_rates(key, part):
    return operator_law(key)[1]


def draw_upper_rates(key, part):
    return operator_law(key)[2]


def draw_cotangent(key, part):
    base_key = jax.random.fold_in(key, 73)
    random_key_list = jax.random.split(base_key, 5)
    axial_pos = (jnp.arange(AXIAL_CELLS, dtype=jnp.float32) + 0.5) / AXIAL_CELLS
    wave_phase = jax.random.uniform(random_key_list[1], (B,), jnp.float32, 0.0, 2.0 * math.pi)
    wave_count = jax.random.uniform(random_key_list[2], (B,), jnp.float32, 0.5, 2.5)
    cross_factor = jax.random.uniform(random_key_list[3], (NY, NZ), jnp.float32, 0.5, 1.5)
    rough_part = jax.random.normal(random_key_list[0], (AXIAL_CELLS, B, NY, NZ), jnp.float32)
    smooth_level = jax.random.uniform(random_key_list[4], (B,), jnp.float32, -1.0, 1.0)
    along_line = smooth_level[None, :] * (1.0 + 0.6 * jnp.sin(2.0 * math.pi * wave_count[None, :] * axial_pos[:, None] + wave_phase[None, :]))
    whole_field = rough_part + along_line[:, :, None, None] * cross_factor[None, None, :, :]
    return jnp.clip(whole_field, -8.0, 8.0)


def touch_ends(result, own_key, least, high):
    shape = result.shape
    place = [jax.random.randint(jax.random.fold_in(own_key, axis), (), 0, shape[axis]) for axis in range(len(shape))]
    result = result.at[tuple(place)].set(least)
    longest = shape.index(max(shape))
    place[longest] = (place[longest] + 1) % shape[longest]
    return result.at[tuple(place)].set(high)


def setup_inputs(seed: int = 0) -> dict:
    splits = jax.random.split(jax.random.key(seed), 9)
    cotangent = draw_cotangent(jax.random.fold_in(splits[8], 71), 0)
    diag_blocks = draw_diag_blocks(jax.random.fold_in(splits[8], 71), 0)
    lower_rates = draw_lower_rates(jax.random.fold_in(splits[8], 71), 0)
    upper_rates = draw_upper_rates(jax.random.fold_in(splits[8], 71), 0)
    cross_rate = jnp.clip(jax.random.uniform(splits[4], (B,), jnp.float32, 0.02, 0.24), 0.02, 0.24)
    bin_profile = jnp.clip(jnp.exp(jax.random.uniform(splits[5], (B,), jnp.float32, math.log(0.1), math.log(1.0))), 0.1, 1.0)
    open_cells = touch_ends((jax.random.randint(splits[6], (NY, NZ), 0, 8) < 7).astype(jnp.int32), jax.random.fold_in(splits[6], 1), 0, 1)
    segment_ids = touch_ends(jax.random.randint(splits[7], (AXIAL_CELLS, NY), 0, SEGMENTS), jax.random.fold_in(splits[7], 1), 0, SEGMENTS - 1).astype(jnp.int32)
    return {"cotangent": cotangent, "diag_blocks": diag_blocks, "lower_rates": lower_rates, "upper_rates": upper_rates, "cross_rate": cross_rate, "bin_profile": bin_profile, "open_cells": open_cells, "segment_ids": segment_ids}


exact_precision = lax.Precision.HIGHEST

def solve_lines(right_side, below_rate, above_rate, adjoint_diag):
    bin_count = right_side.shape[1]
    zero_row = jnp.zeros((1, bin_count), jnp.float32)
    c_prev = jnp.concatenate([zero_row, above_rate[:-1]], axis=0)

    def forward(state_carry, inputs):
        inverse_prev, solve_prev = state_carry
        a_vec, c_last, diag_block, source = inputs
        weight = a_vec[:, None] * inverse_prev
        inverse_now = jnp.linalg.inv(diag_block - weight * c_last[None, :])
        solve_now = source - jnp.matmul(weight, solve_prev, precision=exact_precision)
        return ((inverse_now, solve_now), (inverse_now, solve_now))
    start_state = (jnp.zeros((bin_count, bin_count), jnp.float32), jnp.zeros(right_side.shape[1:], jnp.float32))
    _, (inverses, solves) = lax.scan(forward, start_state, (below_rate, c_prev, adjoint_diag, right_side))

    def backward(next_value, inputs):
        inverse_now, solve_now, c_vec = inputs
        value = jnp.matmul(inverse_now, solve_now - c_vec[:, None] * next_value, precision=exact_precision)
        return (value, value)
    _, values = lax.scan(backward, jnp.zeros(right_side.shape[1:], jnp.float32), (inverses, solves, above_rate), reverse=True)
    return values

def reference(cotangent, diag_blocks, lower_rates, upper_rates, cross_rate, bin_profile, open_cells, segment_ids):
    axial_total, bin_count, rows_all, depth_all = cotangent.shape
    zero_row = jnp.zeros((1, bin_count), jnp.float32)
    below_rate = -jnp.concatenate([zero_row, upper_rates[:-1]], axis=0)
    above_rate = -jnp.concatenate([lower_rates[1:], zero_row], axis=0)
    adjoint_diag = jnp.swapaxes(diag_blocks, 1, 2)
    line_tiles = cotangent.reshape(axial_total, bin_count, N_CROSS, Y_DEV * depth_all)
    line_tiles = jnp.transpose(line_tiles, (2, 0, 1, 3))
    solved = lax.map(lambda tile: solve_lines(tile, below_rate, above_rate, adjoint_diag), line_tiles)
    adjoint = jnp.transpose(solved, (1, 2, 0, 3)).reshape(axial_total, bin_count, rows_all, depth_all)
    open_mask = open_cells.astype(jnp.float32)
    mask_pad = jnp.pad(open_mask, 1)
    field_pad = jnp.pad(adjoint, ((0, 0), (0, 0), (1, 1), (1, 1)))
    flux_sum = jnp.zeros_like(adjoint)
    for shift_y, shift_z in ((0, 1), (2, 1), (1, 0), (1, 2)):
        neighbour_mask = mask_pad[shift_y:shift_y + rows_all, shift_z:shift_z + depth_all]
        neighbour = field_pad[:, :, shift_y:shift_y + rows_all, shift_z:shift_z + depth_all]
        flux_sum = flux_sum + neighbour_mask * (neighbour - adjoint)
    grad_state = adjoint + cross_rate[None, :, None, None] * open_mask * flux_sum
    emitted = jnp.einsum('ibyz,yz->iby', adjoint, open_mask, precision=exact_precision)
    emitted = jnp.einsum('iby,b->iy', emitted, bin_profile, precision=exact_precision) / depth_all
    grad_emission = jax.ops.segment_sum(emitted.reshape(-1), segment_ids.reshape(-1), num_segments=SEGMENTS)
    return (grad_state, grad_emission)
```

```python
import functools

import jax
import jax.numpy as jnp
from jax import lax
from jax.experimental import pallas as pl
from jax.experimental.pallas import tpu as pltpu
from jax.sharding import PartitionSpec as P

SEG_DEV = 4
MESH = pl.DeviceIdType.MESH
exact = lax.Precision.HIGHEST


def dot(a, b):
    return jnp.dot(a, b, precision=exact, preferred_element_type=jnp.float32)


def invert(mats):
    size = mats[0].shape[0]
    row_id = lax.broadcasted_iota(jnp.int32, (size, size), 0)
    col_id = lax.broadcasted_iota(jnp.int32, (size, size), 1)
    for k in range(size):
        done = []
        for a in mats:
            pivot = 1.0 / a[k : k + 1, k : k + 1]
            row = jnp.where(col_id[:1] == k, 1.0, a[k : k + 1, :]) * pivot
            col = a[:, k : k + 1]
            rest = jnp.where(col_id == k, 0.0, a) - col * row
            done.append(jnp.where(row_id == k, row, rest))
        mats = done
    return mats


def kernel(n, nc, cot, diag, low, up, prof_rate, open_ref, out, emit, G, F, X, V, msg_out, msg_in, back_out, back_in,
           edge_out, edge_in, s_msg, r_msg, s_back, r_back, s_hal, r_hal, s_edge, r_edge):
    cells, nb = diag.shape[0], diag.shape[1]
    size = cells * nb
    rows = cot.shape[0] // size
    nz = cot.shape[1]
    per = rows * nz // n
    a = lax.axis_index("axial")
    c = lax.axis_index("cross")
    has_lo = c > 0
    has_hi = c < nc - 1

    barrier = pltpu.get_barrier_semaphore()
    for off in range(1, n):
        pl.semaphore_signal(barrier, inc=1, device_id=(lax.rem(a + off, n), c), device_id_type=MESH)

    @pl.when(has_lo)
    def _():
        pl.semaphore_signal(barrier, inc=1, device_id=(a, c - 1), device_id_type=MESH)

    @pl.when(has_hi)
    def _():
        pl.semaphore_signal(barrier, inc=1, device_id=(a, c + 1), device_id_type=MESH)

    for y in range(rows):
        F[:, (y + 1) * nz : (y + 2) * nz] = cot[pl.ds(y, size, stride=rows), :]

    pl.semaphore_wait(barrier, n - 1 + has_lo.astype(jnp.int32) + has_hi.astype(jnp.int32))

    def hal_copy(down):
        src = F.at[:, nz : 2 * nz] if down else F.at[:, rows * nz : (rows + 1) * nz]
        dst = F.at[:, (rows + 1) * nz : (rows + 2) * nz] if down else F.at[:, 0:nz]
        way = 0 if down else 1
        return pltpu.make_async_remote_copy(
            src_ref=src, dst_ref=dst, send_sem=s_hal.at[way], recv_sem=r_hal.at[way],
            device_id=(a, c - 1 if down else c + 1), device_id_type=MESH)

    def edge_copy(down):
        way = 0 if down else 1
        return pltpu.make_async_remote_copy(
            src_ref=edge_out.at[way], dst_ref=edge_in.at[way], send_sem=s_edge.at[way], recv_sem=r_edge.at[way],
            device_id=(a, c - 1 if down else c + 1), device_id_type=MESH)

    @pl.when(has_lo)
    def _():
        hal_copy(True).start()

    @pl.when(has_hi)
    def _():
        hal_copy(False).start()

    @pl.when(jnp.logical_not(has_lo))
    def _():
        F[:, 0:nz] = jnp.zeros((size, nz), jnp.float32)

    @pl.when(jnp.logical_not(has_hi))
    def _():
        F[:, (rows + 1) * nz : (rows + 2) * nz] = jnp.zeros((size, nz), jnp.float32)

    V[...] = jnp.zeros(V.shape, jnp.float32)
    V[0:cells, 0:nb] = low[...]
    V[cells : 2 * cells, 0:nb] = up[...]
    V[2 * cells : 2 * cells + 2, 0:nb] = prof_rate[...]
    V[...] = V[...].T
    low_col = [V[0:nb, j : j + 1] for j in range(cells)]
    up_col = [V[0:nb, cells + j : cells + j + 1] for j in range(cells)]
    cross_col = V[0:nb, 2 * cells : 2 * cells + 1]
    prof_col = V[0:nb, 2 * cells + 1 : 2 * cells + 2]

    eye = (lax.broadcasted_iota(jnp.int32, (nb, nb), 0) == lax.broadcasted_iota(jnp.int32, (nb, nb), 1)).astype(jnp.float32)

    G[...] = jnp.zeros(G.shape, jnp.float32)
    inverses = invert([diag[i] for i in range(cells)])
    pack = 128 // nb
    same = (lax.broadcasted_iota(jnp.int32, (128, 128), 0) // nb) == (lax.broadcasted_iota(jnp.int32, (128, 128), 1) // nb)
    for g in range(cells // pack):
        tall = jnp.concatenate(inverses[g * pack : (g + 1) * pack], axis=0)
        wide = jnp.where(same, jnp.concatenate([tall] * pack, axis=1), 0.0)
        G[g * 128 : (g + 1) * 128, g * 128 : (g + 1) * 128] = wide.T
    chunk = 1
    while chunk < cells:
        width = chunk * nb
        joints = list(range(chunk, cells, 2 * chunk))
        parts, weights = [], []
        for j in joints:
            o, m = (j - chunk) * nb, j * nb
            lp = up_col[j - 1] * G[m - nb : m, m - nb : m]
            rq = low_col[j] * G[m : m + nb, m : m + nb]
            weights.append(eye - dot(rq, lp))
            parts.append((o, m, lp, rq))
        weights = invert(weights)
        for j, (o, m, lp, rq), w in zip(joints, parts, weights):
            span = max(128, 2 * width)
            lo = o // span * span
            row_l = up_col[j - 1] * G[m - nb : m, lo : lo + span]
            row_r = low_col[j] * G[m : m + nb, lo : lo + span]
            p = dot(w, row_r + dot(rq, row_l))
            q = row_l + dot(lp, p)
            col_l = G[o:m, m - nb : m]
            col_r = G[m : m + width, m : m + nb]
            G[o:m, lo : lo + span] += dot(col_l, p)
            G[m : m + width, lo : lo + span] += dot(col_r, q)
        chunk *= 2

    head, tail = low_col[0], up_col[cells - 1]
    g_head, g_tail = G[0:nb, :], G[size - nb : size, :]
    ends = jnp.concatenate([head * g_head, tail * g_tail], axis=0)
    field = dot(ends, F[:, nz : (rows + 1) * nz])
    ports = jnp.concatenate([ends[:, 0:nb], ends[:, size - nb : size]], axis=1)
    for e in range(n):
        bits = [ports, field[:, e * per : (e + 1) * per]]
        if 2 * nb + per < 128:
            bits.append(jnp.zeros((2 * nb, 128 - 2 * nb - per), jnp.float32))
        msg_out[e] = jnp.concatenate(bits, axis=1)

    def msg_copy(off):
        peer = lax.rem(a + off, n)
        return pltpu.make_async_remote_copy(
            src_ref=msg_out.at[peer], dst_ref=msg_in.at[a], send_sem=s_msg.at[off], recv_sem=r_msg.at[off],
            device_id=(peer, c), device_id_type=MESH)

    def back_copy(off):
        peer = lax.rem(a + off, n)
        return pltpu.make_async_remote_copy(
            src_ref=back_out.at[peer], dst_ref=back_in.at[a], send_sem=s_back.at[off], recv_sem=r_back.at[off],
            device_id=(peer, c), device_id_type=MESH)

    for off in range(1, n):
        msg_copy(off).start()
    msg_in[a] = msg_out[a]

    half = rows * nz // 2
    for part in range(2):
        X[:, nz + part * half : nz + (part + 1) * half] = dot(G[...], F[:, nz + part * half : nz + (part + 1) * half])

    @pl.when(has_lo)
    def _():
        hal_copy(True).wait_send()
        hal_copy(False).wait_recv()

    @pl.when(has_hi)
    def _():
        hal_copy(False).wait_send()
        hal_copy(True).wait_recv()

    sides = dot(G[...], jnp.concatenate([F[:, 0:nz], F[:, (rows + 1) * nz : (rows + 2) * nz]], axis=1))
    X[:, 0:nz] = sides[:, 0:nz]
    X[:, (rows + 1) * nz : (rows + 2) * nz] = sides[:, nz : 2 * nz]

    for off in range(1, n):
        msg_copy(off).wait_recv()

    lane = lax.broadcasted_iota(jnp.int32, (1, 128), 1)
    keep_l = jnp.where((lane >= nb) & (lane < 2 * nb), 0.0, 1.0)
    keep_r = jnp.where(lane < nb, 0.0, 1.0)
    groups = [(msg_in[d][0:nb], msg_in[d][nb : 2 * nb], None) for d in range(n)]
    while len(groups) > 1:
        pairs = [(groups[i], groups[i + 1]) for i in range(0, len(groups), 2)]
        weights = invert([eye - dot(r[0][:, 0:nb], l[1][:, nb : 2 * nb]) for l, r in pairs])
        top = len(pairs) == 1
        groups = []
        for (l, r), w in zip(pairs, weights):
            from_l, from_r = l[1] * keep_l, r[0] * keep_r
            p = dot(w, from_r + dot(r[0][:, 0:nb], from_l))
            q = from_l + dot(l[1][:, nb : 2 * nb], p)
            left = l[0] if l[2] is None else jnp.concatenate([l[0], l[2]], axis=0)
            right = r[1] if r[2] is None else jnp.concatenate([r[1], r[2]], axis=0)
            left = left * keep_l + dot(left[:, nb : 2 * nb], p)
            right = right * keep_r + dot(right[:, 0:nb], q)
            inner = [p, q]
            if l[2] is not None:
                inner = [left[nb:]] + inner
            if r[2] is not None:
                inner = inner + [right[nb:]]
            groups.append((left[0:nb], right[0:nb], jnp.concatenate(inner, axis=0)))
    inner = groups[0][2]
    none = jnp.zeros((nb, 128), jnp.float32)
    for d in range(n):
        if d == 0:
            back_out[d] = jnp.concatenate([none, inner[0:nb]], axis=0)
        elif d == n - 1:
            back_out[d] = jnp.concatenate([inner[(2 * d - 1) * nb :], none], axis=0)
        else:
            back_out[d] = inner[(2 * d - 1) * nb : (2 * d + 1) * nb]
    for off in range(1, n):
        back_copy(off).start()
    back_in[a] = back_out[a]
    for off in range(1, n):
        back_copy(off).wait_recv()

    each = n // rows
    flux = []
    for y in range(rows):
        flux.append(jnp.concatenate([back_in[y * each + e][:, 2 * nb : 2 * nb + per] for e in range(each)], axis=1))
    edge_out[0] = flux[0]
    edge_out[1] = flux[rows - 1]

    @pl.when(has_lo)
    def _():
        edge_copy(True).start()

    @pl.when(has_hi)
    def _():
        edge_copy(False).start()

    gc = jnp.concatenate([G[:, 0:nb], G[:, size - nb : size]], axis=1)
    X[:, nz : (rows + 1) * nz] += dot(gc, jnp.concatenate(flux, axis=1))

    @pl.when(has_lo)
    def _():
        edge_copy(True).wait_send()
        edge_copy(False).wait_recv()
        X[:, 0:nz] += dot(gc, edge_in[1])

    @pl.when(has_hi)
    def _():
        edge_copy(False).wait_send()
        edge_copy(True).wait_recv()
        X[:, (rows + 1) * nz : (rows + 2) * nz] += dot(gc, edge_in[0])

    opens = []
    for y in range(-1, rows + 1):
        at = jnp.clip(c * rows + y, 0, nc * rows - 1)
        line = open_ref[pl.ds(at, 1), :].astype(jnp.float32)
        if y == -1:
            line = jnp.where(has_lo, line, 0.0)
        if y == rows:
            line = jnp.where(has_hi, line, 0.0)
        opens.append(line)
    zlane = lax.broadcasted_iota(jnp.int32, (1, nz), 1)
    step_col = jnp.concatenate([cross_col] * 4, axis=0)
    share_col = jnp.concatenate([prof_col] * 4, axis=0)
    block = 4 * nb
    for y in range(rows):
        here = opens[y + 1]
        before = jnp.where(zlane == 0, 0.0, pltpu.roll(here, 1, 1)) * here
        after = jnp.where(zlane == nz - 1, 0.0, pltpu.roll(here, nz - 1, 1)) * here
        above = opens[y] * here
        below = opens[y + 2] * here
        total = before + after + above + below
        for i in range(size // block):
            at = slice(i * block, (i + 1) * block)
            x = X[at, (y + 1) * nz : (y + 2) * nz]
            moved = (above * (X[at, y * nz : (y + 1) * nz] - x) + below * (X[at, (y + 2) * nz : (y + 3) * nz] - x)
                     + before * (pltpu.roll(x, 1, 1) - x) + after * (pltpu.roll(x, nz - 1, 1) - x))
            out[pl.ds(i * block * rows + y, block, stride=rows), :] = x + step_col * moved
            sent = x * here * share_col
            for k in range(4):
                emit[y, pl.ds(i * 4 + k, 1), :] = jnp.sum(sent[k * nb : (k + 1) * nb], axis=0, keepdims=True)

    for off in range(1, n):
        msg_copy(off).wait_send()
        back_copy(off).wait_send()


def per_device(n, nc, cotangent, diag_blocks, lower_rates, upper_rates, cross_rate, bin_profile, open_cells, segment_ids):
    cells, nb, rows, nz = cotangent.shape
    size = cells * nb
    vmem = pl.BlockSpec(memory_space=pltpu.VMEM)
    dma = pltpu.SemaphoreType.DMA
    grad, emit = pl.pallas_call(
        functools.partial(kernel, n, nc),
        out_shape=(
            jax.ShapeDtypeStruct((size * rows, nz), jnp.float32),
            jax.ShapeDtypeStruct((rows, cells, nz), jnp.float32),
        ),
        in_specs=[vmem] * 6,
        out_specs=(vmem, vmem),
        scratch_shapes=[
            pltpu.VMEM((size, size), jnp.float32),
            pltpu.VMEM((size, (rows + 2) * nz), jnp.float32),
            pltpu.VMEM((size, (rows + 2) * nz), jnp.float32),
            pltpu.VMEM((128, 128), jnp.float32),
            pltpu.VMEM((n, 2 * nb, 128), jnp.float32),
            pltpu.VMEM((n, 2 * nb, 128), jnp.float32),
            pltpu.VMEM((n, 2 * nb, 128), jnp.float32),
            pltpu.VMEM((n, 2 * nb, 128), jnp.float32),
            pltpu.VMEM((2, 2 * nb, nz), jnp.float32),
            pltpu.VMEM((2, 2 * nb, nz), jnp.float32),
            dma((n,)), dma((n,)), dma((n,)), dma((n,)), dma((2,)), dma((2,)), dma((2,)), dma((2,)),
        ],
        compiler_params=pltpu.CompilerParams(
            collective_id=0, has_side_effects=True, vmem_limit_bytes=48 * 1024 * 1024
        ),
    )(
        cotangent.reshape(size * rows, nz), diag_blocks, lower_rates, upper_rates,
        jnp.stack([cross_rate, bin_profile]), open_cells,
    )
    emitted = jnp.sum(emit, axis=-1).T / nz
    wanted = lax.iota(jnp.int32, SEG_DEV * n * nc)
    onehot = (segment_ids.reshape(-1)[:, None] == wanted[None, :]).astype(jnp.float32)
    grad_emission = lax.psum_scatter(
        jnp.dot(emitted.reshape(-1), onehot, precision=exact), ("axial", "cross"), scatter_dimension=0, tiled=True
    )
    return grad.reshape(cotangent.shape), grad_emission


def solution(mesh):
    in_specs = (
        P("axial", None, "cross", None),
        P("axial", None, None),
        P("axial", None),
        P("axial", None),
        P(),
        P(),
        P(),
        P("axial", "cross"),
    )
    out_specs = (P("axial", None, "cross", None), P(("axial", "cross")))
    return jax.shard_map(
        functools.partial(per_device, mesh.shape["axial"], mesh.shape["cross"]),
        mesh=mesh, in_specs=in_specs, out_specs=out_specs, check_vma=False,
    )
```

```python
import functools

import jax
import jax.numpy as jnp
from jax import lax
from jax.experimental import pallas as pl
from jax.experimental.pallas import tpu as pltpu
from jax.sharding import PartitionSpec as P

SEG_DEV = 4
MESH = pl.DeviceIdType.MESH
exact = lax.Precision.HIGHEST


def dot(a, b):
    return jnp.dot(a, b, precision=exact, preferred_element_type=jnp.float32)


def invert(mats):
    size = mats[0].shape[0]
    row_id = lax.broadcasted_iota(jnp.int32, (size, size), 0)
    col_id = lax.broadcasted_iota(jnp.int32, (size, size), 1)
    for k in range(size):
        done = []
        for a in mats:
            pivot = 1.0 / a[k : k + 1, k : k + 1]
            row = jnp.where(col_id[:1] == k, 1.0, a[k : k + 1, :]) * pivot
            col = a[:, k : k + 1]
            rest = jnp.where(col_id == k, 0.0, a) - col * row
            done.append(jnp.where(row_id == k, row, rest))
        mats = done
    return mats


def kernel(n, nc, cot_hbm, diag_hbm, low_hbm, up_hbm, cross_hbm, prof_hbm, open_hbm, seg_hbm, out, out_seg,
           cot, diag, low, up, cross_rate, prof_rate, open_ref, seg, G, F, X, V, msg_out, msg_in, back_out, back_in,
           edge_out, edge_in, sum_out, sum_cross, sum_axial, s_in, s_msg, r_msg, s_back, r_back, s_hal, r_hal,
           s_edge, r_edge, s_cross, r_cross, s_axial, r_axial):
    pairs_in = [(cot_hbm, cot), (diag_hbm, diag), (low_hbm, low), (up_hbm, up), (cross_hbm, cross_rate), (prof_hbm, prof_rate),
                (open_hbm, open_ref), (seg_hbm, seg)]
    loads = [pltpu.make_async_copy(src, dst, s_in.at[i]) for i, (src, dst) in enumerate(pairs_in)]
    for i in (1, 0, 2, 3, 4, 5, 6, 7):
        loads[i].start()
    cells, nb = diag.shape[0], diag.shape[1]
    size = cells * nb
    rows = cot.shape[0] // size
    nz = cot.shape[1]
    per = rows * nz // n
    a = lax.axis_index("axial")
    c = lax.axis_index("cross")
    has_lo = c > 0
    has_hi = c < nc - 1

    barrier = pltpu.get_barrier_semaphore()
    for off in range(1, n):
        pl.semaphore_signal(barrier, inc=1, device_id=(lax.rem(a + off, n), c), device_id_type=MESH)

    for off in range(1, nc):
        pl.semaphore_signal(barrier, inc=1, device_id=(a, lax.rem(c + off, nc)), device_id_type=MESH)

    loads[1].wait()
    inverses = invert([diag[i] for i in range(cells)])

    loads[0].wait()
    for y in range(rows):
        F[:, (y + 1) * nz : (y + 2) * nz] = cot[pl.ds(y, size, stride=rows), :]

    pl.semaphore_wait(barrier, n - 1 + nc - 1)

    def hal_copy(down):
        src = F.at[:, nz : 2 * nz] if down else F.at[:, rows * nz : (rows + 1) * nz]
        dst = F.at[:, (rows + 1) * nz : (rows + 2) * nz] if down else F.at[:, 0:nz]
        way = 0 if down else 1
        return pltpu.make_async_remote_copy(
            src_ref=src, dst_ref=dst, send_sem=s_hal.at[way], recv_sem=r_hal.at[way],
            device_id=(a, c - 1 if down else c + 1), device_id_type=MESH)

    def edge_copy(down):
        way = 0 if down else 1
        return pltpu.make_async_remote_copy(
            src_ref=edge_out.at[way], dst_ref=edge_in.at[way], send_sem=s_edge.at[way], recv_sem=r_edge.at[way],
            device_id=(a, c - 1 if down else c + 1), device_id_type=MESH)

    @pl.when(has_lo)
    def _():
        hal_copy(True).start()

    @pl.when(has_hi)
    def _():
        hal_copy(False).start()

    @pl.when(jnp.logical_not(has_lo))
    def _():
        F[:, 0:nz] = jnp.zeros((size, nz), jnp.float32)

    @pl.when(jnp.logical_not(has_hi))
    def _():
        F[:, (rows + 1) * nz : (rows + 2) * nz] = jnp.zeros((size, nz), jnp.float32)

    for i in range(2, 8):
        loads[i].wait()
    V[...] = jnp.zeros(V.shape, jnp.float32)
    V[0:cells, 0:nb] = low[...]
    V[cells : 2 * cells, 0:nb] = up[...]
    V[2 * cells : 2 * cells + 1, 0:nb] = cross_rate[...]
    V[2 * cells + 1 : 2 * cells + 2, 0:nb] = prof_rate[...]
    V[2 * cells + 2 : 2 * cells + 2 + rows, 0:cells] = seg[...].astype(jnp.float32)
    V[...] = V[...].T
    low_col = [V[0:nb, j : j + 1] for j in range(cells)]
    up_col = [V[0:nb, cells + j : cells + j + 1] for j in range(cells)]
    cross_col = V[0:nb, 2 * cells : 2 * cells + 1]
    prof_col = V[0:nb, 2 * cells + 1 : 2 * cells + 2]
    seg_col = [V[0:cells, 2 * cells + 2 + y : 2 * cells + 3 + y] for y in range(rows)]

    eye = (lax.broadcasted_iota(jnp.int32, (nb, nb), 0) == lax.broadcasted_iota(jnp.int32, (nb, nb), 1)).astype(jnp.float32)

    G[...] = jnp.zeros(G.shape, jnp.float32)
    pack = 128 // nb
    same = (lax.broadcasted_iota(jnp.int32, (128, 128), 0) // nb) == (lax.broadcasted_iota(jnp.int32, (128, 128), 1) // nb)
    for g in range(cells // pack):
        tall = jnp.concatenate(inverses[g * pack : (g + 1) * pack], axis=0)
        wide = jnp.where(same, jnp.concatenate([tall] * pack, axis=1), 0.0)
        G[g * 128 : (g + 1) * 128, g * 128 : (g + 1) * 128] = wide.T
    chunk = 1
    while chunk < cells:
        width = chunk * nb
        joints = list(range(chunk, cells, 2 * chunk))
        parts, weights = [], []
        for j in joints:
            o, m = (j - chunk) * nb, j * nb
            lp = up_col[j - 1] * G[m - nb : m, m - nb : m]
            rq = low_col[j] * G[m : m + nb, m : m + nb]
            weights.append(eye - dot(rq, lp))
            parts.append((o, m, lp, rq))
        weights = invert(weights)
        for j, (o, m, lp, rq), w in zip(joints, parts, weights):
            span = max(128, 2 * width)
            lo = o // span * span
            row_l = up_col[j - 1] * G[m - nb : m, lo : lo + span]
            row_r = low_col[j] * G[m : m + nb, lo : lo + span]
            p = dot(w, row_r + dot(rq, row_l))
            q = row_l + dot(lp, p)
            col_l = G[o:m, m - nb : m]
            col_r = G[m : m + width, m : m + nb]
            G[o:m, lo : lo + span] += dot(col_l, p)
            G[m : m + width, lo : lo + span] += dot(col_r, q)
        chunk *= 2

    head, tail = low_col[0], up_col[cells - 1]
    g_head, g_tail = G[0:nb, :], G[size - nb : size, :]
    ends = jnp.concatenate([head * g_head, tail * g_tail], axis=0)
    field = dot(ends, F[:, nz : (rows + 1) * nz])
    ports = jnp.concatenate([ends[:, 0:nb], ends[:, size - nb : size]], axis=1)
    for e in range(n):
        bits = [ports, field[:, e * per : (e + 1) * per]]
        if 2 * nb + per < 128:
            bits.append(jnp.zeros((2 * nb, 128 - 2 * nb - per), jnp.float32))
        msg_out[e] = jnp.concatenate(bits, axis=1)

    def msg_copy(off):
        peer = lax.rem(a + off, n)
        return pltpu.make_async_remote_copy(
            src_ref=msg_out.at[peer], dst_ref=msg_in.at[a], send_sem=s_msg.at[off], recv_sem=r_msg.at[off],
            device_id=(peer, c), device_id_type=MESH)

    def back_copy(off):
        peer = lax.rem(a + off, n)
        return pltpu.make_async_remote_copy(
            src_ref=back_out.at[peer], dst_ref=back_in.at[a], send_sem=s_back.at[off], recv_sem=r_back.at[off],
            device_id=(peer, c), device_id_type=MESH)

    for off in range(1, n):
        msg_copy(off).start()
    msg_in[a] = msg_out[a]

    half = rows * nz // 2
    for part in range(2):
        X[:, nz + part * half : nz + (part + 1) * half] = dot(G[...], F[:, nz + part * half : nz + (part + 1) * half])

    @pl.when(has_lo)
    def _():
        hal_copy(True).wait_send()
        hal_copy(False).wait_recv()

    @pl.when(has_hi)
    def _():
        hal_copy(False).wait_send()
        hal_copy(True).wait_recv()

    sides = dot(G[...], jnp.concatenate([F[:, 0:nz], F[:, (rows + 1) * nz : (rows + 2) * nz]], axis=1))
    X[:, 0:nz] = sides[:, 0:nz]
    X[:, (rows + 1) * nz : (rows + 2) * nz] = sides[:, nz : 2 * nz]

    for off in range(1, n):
        msg_copy(off).wait_recv()

    lane = lax.broadcasted_iota(jnp.int32, (1, 128), 1)
    keep_l = jnp.where((lane >= nb) & (lane < 2 * nb), 0.0, 1.0)
    keep_r = jnp.where(lane < nb, 0.0, 1.0)
    groups = [(msg_in[d][0:nb], msg_in[d][nb : 2 * nb], None) for d in range(n)]
    while len(groups) > 1:
        pairs = [(groups[i], groups[i + 1]) for i in range(0, len(groups), 2)]
        weights = invert([eye - dot(r[0][:, 0:nb], l[1][:, nb : 2 * nb]) for l, r in pairs])
        top = len(pairs) == 1
        groups = []
        for (l, r), w in zip(pairs, weights):
            from_l, from_r = l[1] * keep_l, r[0] * keep_r
            p = dot(w, from_r + dot(r[0][:, 0:nb], from_l))
            q = from_l + dot(l[1][:, nb : 2 * nb], p)
            left = l[0] if l[2] is None else jnp.concatenate([l[0], l[2]], axis=0)
            right = r[1] if r[2] is None else jnp.concatenate([r[1], r[2]], axis=0)
            left = left * keep_l + dot(left[:, nb : 2 * nb], p)
            right = right * keep_r + dot(right[:, 0:nb], q)
            inner = [p, q]
            if l[2] is not None:
                inner = [left[nb:]] + inner
            if r[2] is not None:
                inner = inner + [right[nb:]]
            groups.append((left[0:nb], right[0:nb], jnp.concatenate(inner, axis=0)))
    inner = groups[0][2]
    none = jnp.zeros((nb, 128), jnp.float32)
    for d in range(n):
        if d == 0:
            back_out[d] = jnp.concatenate([none, inner[0:nb]], axis=0)
        elif d == n - 1:
            back_out[d] = jnp.concatenate([inner[(2 * d - 1) * nb :], none], axis=0)
        else:
            back_out[d] = inner[(2 * d - 1) * nb : (2 * d + 1) * nb]
    for off in range(1, n):
        back_copy(off).start()
    back_in[a] = back_out[a]
    for off in range(1, n):
        back_copy(off).wait_recv()

    each = n // rows
    flux = []
    for y in range(rows):
        flux.append(jnp.concatenate([back_in[y * each + e][:, 2 * nb : 2 * nb + per] for e in range(each)], axis=1))
    edge_out[0] = flux[0]
    edge_out[1] = flux[rows - 1]

    @pl.when(has_lo)
    def _():
        edge_copy(True).start()

    @pl.when(has_hi)
    def _():
        edge_copy(False).start()

    gc = jnp.concatenate([G[:, 0:nb], G[:, size - nb : size]], axis=1)
    X[:, nz : (rows + 1) * nz] += dot(gc, jnp.concatenate(flux, axis=1))

    opens = []
    for y in range(-1, rows + 1):
        at = jnp.clip(c * rows + y, 0, nc * rows - 1)
        line = open_ref[pl.ds(at, 1), :].astype(jnp.float32)
        if y == -1:
            line = jnp.where(has_lo, line, 0.0)
        if y == rows:
            line = jnp.where(has_hi, line, 0.0)
        opens.append(line)

    segs = sum_out.shape[-1]
    seg_id = lax.broadcasted_iota(jnp.int32, (1, segs), 1)
    gain = jnp.zeros((8, segs), jnp.float32)
    for y in range(rows):
        bits = []
        for i in range(cells):
            sent = X[i * nb : (i + 1) * nb, (y + 1) * nz : (y + 2) * nz] * prof_col
            bits.append(jnp.sum(sent, axis=0, keepdims=True))
        given = jnp.sum(jnp.concatenate(bits, axis=0) * opens[y + 1], axis=1, keepdims=True) * (1.0 / nz)
        picked = jnp.where(seg_col[y] == seg_id.astype(jnp.float32), given, 0.0)
        for i in range(cells // 8):
            gain = gain + picked[i * 8 : (i + 1) * 8]
    sum_out[0] = gain

    def cross_copy(off):
        return pltpu.make_async_remote_copy(
            src_ref=sum_out.at[0], dst_ref=sum_cross.at[off], send_sem=s_cross.at[off], recv_sem=r_cross.at[off],
            device_id=(a, lax.rem(c + off, nc)), device_id_type=MESH)

    def axial_copy(off):
        return pltpu.make_async_remote_copy(
            src_ref=sum_out.at[1], dst_ref=sum_axial.at[off], send_sem=s_axial.at[off], recv_sem=r_axial.at[off],
            device_id=(lax.rem(a + off, n), c), device_id_type=MESH)

    for off in range(1, nc):
        cross_copy(off).start()

    @pl.when(has_lo)
    def _():
        edge_copy(True).wait_send()
        edge_copy(False).wait_recv()
        X[:, 0:nz] += dot(gc, edge_in[1])

    @pl.when(has_hi)
    def _():
        edge_copy(False).wait_send()
        edge_copy(True).wait_recv()
        X[:, (rows + 1) * nz : (rows + 2) * nz] += dot(gc, edge_in[0])

    zlane = lax.broadcasted_iota(jnp.int32, (1, nz), 1)
    step_col = jnp.concatenate([cross_col] * 4, axis=0)
    block = 4 * nb
    for y in range(rows):
        here = opens[y + 1]
        before = jnp.where(zlane == 0, 0.0, pltpu.roll(here, 1, 1)) * here
        after = jnp.where(zlane == nz - 1, 0.0, pltpu.roll(here, nz - 1, 1)) * here
        above = opens[y] * here
        below = opens[y + 2] * here
        total = before + after + above + below
        for i in range(size // block):
            at = slice(i * block, (i + 1) * block)
            x = X[at, (y + 1) * nz : (y + 2) * nz]
            moved = (above * (X[at, y * nz : (y + 1) * nz] - x) + below * (X[at, (y + 2) * nz : (y + 3) * nz] - x)
                     + before * (pltpu.roll(x, 1, 1) - x) + after * (pltpu.roll(x, nz - 1, 1) - x))
            out[pl.ds(i * block * rows + y, block, stride=rows), :] = x + step_col * moved
        if y == 0:
            gain = sum_out[0]
            for off in range(1, nc):
                cross_copy(off).wait_recv()
                gain = gain + sum_cross[off]
            sum_out[1] = gain
            for off in range(1, n):
                axial_copy(off).start()

    gain = sum_out[1]
    for off in range(1, n):
        axial_copy(off).wait_recv()
        gain = gain + sum_axial[off]
    gain = jnp.sum(gain, axis=0, keepdims=True)
    own = out_seg.shape[1]
    own_id = lax.broadcasted_iota(jnp.int32, (1, own), 1)
    result = jnp.zeros((1, own), jnp.float32)
    for j in range(own):
        mine = jnp.sum(jnp.where(seg_id == (a * nc + c) * own + j, gain, 0.0), axis=1, keepdims=True)
        result = jnp.where(own_id == j, mine, result)
    out_seg[...] = result

    for off in range(1, nc):
        cross_copy(off).wait_send()
    for off in range(1, n):
        axial_copy(off).wait_send()

    for off in range(1, n):
        msg_copy(off).wait_send()
        back_copy(off).wait_send()


def per_device(n, nc, cotangent, diag_blocks, lower_rates, upper_rates, cross_rate, bin_profile, open_cells, segment_ids):
    cells, nb, rows, nz = cotangent.shape
    size = cells * nb
    segs = SEG_DEV * n * nc
    vmem = pl.BlockSpec(memory_space=pltpu.VMEM)
    hbm = pl.BlockSpec(memory_space=pltpu.HBM)
    dma = pltpu.SemaphoreType.DMA
    f32 = jnp.float32
    operands = (
        cotangent.reshape(size * rows, nz), diag_blocks, lower_rates, upper_rates,
        cross_rate.reshape(1, nb), bin_profile.reshape(1, nb), open_cells, segment_ids.T,
    )
    grad, gain = pl.pallas_call(
        functools.partial(kernel, n, nc),
        out_shape=(jax.ShapeDtypeStruct((size * rows, nz), f32), jax.ShapeDtypeStruct((1, SEG_DEV), f32)),
        in_specs=[hbm] * len(operands),
        out_specs=(vmem, vmem),
        scratch_shapes=[pltpu.VMEM(x.shape, x.dtype) for x in operands] + [
            pltpu.VMEM((size, size), f32),
            pltpu.VMEM((size, (rows + 2) * nz), f32),
            pltpu.VMEM((size, (rows + 2) * nz), f32),
            pltpu.VMEM((128, 128), f32),
            pltpu.VMEM((n, 2 * nb, 128), f32),
            pltpu.VMEM((n, 2 * nb, 128), f32),
            pltpu.VMEM((n, 2 * nb, 128), f32),
            pltpu.VMEM((n, 2 * nb, 128), f32),
            pltpu.VMEM((2, 2 * nb, nz), f32),
            pltpu.VMEM((2, 2 * nb, nz), f32),
            pltpu.VMEM((2, 8, segs), f32),
            pltpu.VMEM((nc, 8, segs), f32),
            pltpu.VMEM((n, 8, segs), f32),
            dma((len(operands),)), dma((n,)), dma((n,)), dma((n,)), dma((n,)), dma((2,)), dma((2,)), dma((2,)), dma((2,)),
            dma((nc,)), dma((nc,)), dma((n,)), dma((n,)),
        ],
        compiler_params=pltpu.CompilerParams(
            collective_id=0, has_side_effects=True, vmem_limit_bytes=63 * 1024 * 1024 + 512 * 1024
        ),
    )(*operands)
    return grad.reshape(cotangent.shape), gain.reshape(SEG_DEV)


def solution(mesh):
    in_specs = (
        P("axial", None, "cross", None),
        P("axial", None, None),
        P("axial", None),
        P("axial", None),
        P(),
        P(),
        P(),
        P("axial", "cross"),
    )
    out_specs = (P("axial", None, "cross", None), P(("axial", "cross")))
    return jax.shard_map(
        functools.partial(per_device, mesh.shape["axial"], mesh.shape["cross"]),
        mesh=mesh, in_specs=in_specs, out_specs=out_specs, check_vma=False,
    )
```

```python
import functools

import jax
import jax.numpy as jnp
from jax import lax
from jax.experimental import pallas as pl
from jax.experimental.pallas import tpu as pltpu
from jax.sharding import PartitionSpec as P

SEG_DEV = 4
PANEL_FEW = 8
PANEL_MANY = 4
MESH = pl.DeviceIdType.MESH
exact = lax.Precision.HIGHEST


def dot(a, b):
    return jnp.dot(a, b, precision=exact, preferred_element_type=jnp.float32)


def invert(mats):
    size = mats[0].shape[0]
    panel = PANEL_FEW if len(mats) <= 4 else PANEL_MANY
    slabs = range(size // 8)
    row_id = lax.broadcasted_iota(jnp.int32, (8, size), 0)
    col_id = lax.broadcasted_iota(jnp.int32, (8, size), 1)
    mats = [[a[s * 8 : (s + 1) * 8] for s in slabs] for a in mats]
    for first in range(0, size, panel):
        spread = [
            [[jnp.broadcast_to(a[s][:, first + j : first + j + 1], (8, size)) for s in slabs] for j in range(panel)]
            for a in mats
        ]
        for j in range(panel):
            k = first + j
            home, at = k // 8, k % 8
            for i, a in enumerate(mats):
                col = spread[i][j]
                pivot = 1.0 / col[home][at : at + 1]
                row = jnp.where(col_id[:1] == k, 1.0, a[home][at : at + 1]) * pivot
                done = [jnp.where(col_id == k, 0.0, a[s]) - col[s] * row for s in slabs]
                done[home] = jnp.where(row_id == at, row, done[home])
                mats[i] = done
                for m in range(j + 1, panel):
                    other = spread[i][m]
                    entry = other[home][at : at + 1] * pivot
                    later = [other[s] - col[s] * entry for s in slabs]
                    later[home] = jnp.where(row_id == at, entry, later[home])
                    spread[i][m] = later
    return [jnp.concatenate(a, axis=0) for a in mats]


def kernel(n, nc, cot_hbm, diag_hbm, low_hbm, up_hbm, cross_hbm, prof_hbm, open_hbm, seg_hbm, out, out_seg,
           cot, diag, low, up, cross_rate, prof_rate, open_ref, seg, G, F, X, V, msg_out, msg_in, back_out, back_in,
           edge_out, edge_in, sum_out, sum_cross, sum_axial, s_in, s_msg, r_msg, s_back, r_back, s_hal, r_hal,
           s_edge, r_edge, s_cross, r_cross, s_axial, r_axial):
    pairs_in = [(cot_hbm, cot), (diag_hbm, diag), (low_hbm, low), (up_hbm, up), (cross_hbm, cross_rate), (prof_hbm, prof_rate),
                (open_hbm, open_ref), (seg_hbm, seg)]
    loads = [pltpu.make_async_copy(src, dst, s_in.at[i]) for i, (src, dst) in enumerate(pairs_in)]
    for i in (1, 0, 2, 3, 4, 5, 6, 7):
        loads[i].start()
    cells, nb = diag.shape[0], diag.shape[1]
    size = cells * nb
    rows = cot.shape[0] // size
    nz = cot.shape[1]
    per = rows * nz // n
    a = lax.axis_index("axial")
    c = lax.axis_index("cross")
    has_lo = c > 0
    has_hi = c < nc - 1

    barrier = pltpu.get_barrier_semaphore()
    for off in range(1, n):
        pl.semaphore_signal(barrier, inc=1, device_id=(lax.rem(a + off, n), c), device_id_type=MESH)

    for off in range(1, nc):
        pl.semaphore_signal(barrier, inc=1, device_id=(a, lax.rem(c + off, nc)), device_id_type=MESH)

    loads[1].wait()
    inverses = invert([diag[i] for i in range(cells)])

    loads[0].wait()
    for y in range(rows):
        F[:, (y + 1) * nz : (y + 2) * nz] = cot[pl.ds(y, size, stride=rows), :]

    pl.semaphore_wait(barrier, n - 1 + nc - 1)

    def hal_copy(down):
        src = F.at[:, nz : 2 * nz] if down else F.at[:, rows * nz : (rows + 1) * nz]
        dst = F.at[:, (rows + 1) * nz : (rows + 2) * nz] if down else F.at[:, 0:nz]
        way = 0 if down else 1
        return pltpu.make_async_remote_copy(
            src_ref=src, dst_ref=dst, send_sem=s_hal.at[way], recv_sem=r_hal.at[way],
            device_id=(a, c - 1 if down else c + 1), device_id_type=MESH)

    def edge_copy(down):
        way = 0 if down else 1
        return pltpu.make_async_remote_copy(
            src_ref=edge_out.at[way], dst_ref=edge_in.at[way], send_sem=s_edge.at[way], recv_sem=r_edge.at[way],
            device_id=(a, c - 1 if down else c + 1), device_id_type=MESH)

    @pl.when(has_lo)
    def _():
        hal_copy(True).start()

    @pl.when(has_hi)
    def _():
        hal_copy(False).start()

    @pl.when(jnp.logical_not(has_lo))
    def _():
        F[:, 0:nz] = jnp.zeros((size, nz), jnp.float32)

    @pl.when(jnp.logical_not(has_hi))
    def _():
        F[:, (rows + 1) * nz : (rows + 2) * nz] = jnp.zeros((size, nz), jnp.float32)

    for i in range(2, 8):
        loads[i].wait()
    V[...] = jnp.zeros(V.shape, jnp.float32)
    V[0:cells, 0:nb] = low[...]
    V[cells : 2 * cells, 0:nb] = up[...]
    V[2 * cells : 2 * cells + 1, 0:nb] = cross_rate[...]
    V[2 * cells + 1 : 2 * cells + 2, 0:nb] = prof_rate[...]
    V[2 * cells + 2 : 2 * cells + 2 + rows, 0:cells] = seg[...].astype(jnp.float32)
    V[...] = V[...].T
    low_col = [V[0:nb, j : j + 1] for j in range(cells)]
    up_col = [V[0:nb, cells + j : cells + j + 1] for j in range(cells)]
    cross_col = V[0:nb, 2 * cells : 2 * cells + 1]
    prof_col = V[0:nb, 2 * cells + 1 : 2 * cells + 2]
    seg_col = [V[0:cells, 2 * cells + 2 + y : 2 * cells + 3 + y] for y in range(rows)]

    eye = (lax.broadcasted_iota(jnp.int32, (nb, nb), 0) == lax.broadcasted_iota(jnp.int32, (nb, nb), 1)).astype(jnp.float32)

    G[...] = jnp.zeros(G.shape, jnp.float32)
    pack = 128 // nb
    same = (lax.broadcasted_iota(jnp.int32, (128, 128), 0) // nb) == (lax.broadcasted_iota(jnp.int32, (128, 128), 1) // nb)
    for g in range(cells // pack):
        tall = jnp.concatenate(inverses[g * pack : (g + 1) * pack], axis=0)
        wide = jnp.where(same, jnp.concatenate([tall] * pack, axis=1), 0.0)
        G[g * 128 : (g + 1) * 128, g * 128 : (g + 1) * 128] = wide.T
    chunk = 1
    while chunk < cells:
        width = chunk * nb
        joints = list(range(chunk, cells, 2 * chunk))
        parts, weights = [], []
        for j in joints:
            o, m = (j - chunk) * nb, j * nb
            lp = up_col[j - 1] * G[m - nb : m, m - nb : m]
            rq = low_col[j] * G[m : m + nb, m : m + nb]
            weights.append(eye - dot(rq, lp))
            parts.append((o, m, lp, rq))
        weights = invert(weights)
        for j, (o, m, lp, rq), w in zip(joints, parts, weights):
            span = max(128, 2 * width)
            lo = o // span * span
            row_l = up_col[j - 1] * G[m - nb : m, lo : lo + span]
            row_r = low_col[j] * G[m : m + nb, lo : lo + span]
            p = dot(w, row_r + dot(rq, row_l))
            q = row_l + dot(lp, p)
            col_l = G[o:m, m - nb : m]
            col_r = G[m : m + width, m : m + nb]
            G[o:m, lo : lo + span] += dot(col_l, p)
            G[m : m + width, lo : lo + span] += dot(col_r, q)
        chunk *= 2

    head, tail = low_col[0], up_col[cells - 1]
    g_head, g_tail = G[0:nb, :], G[size - nb : size, :]
    ends = jnp.concatenate([head * g_head, tail * g_tail], axis=0)
    field = dot(ends, F[:, nz : (rows + 1) * nz])
    ports = jnp.concatenate([ends[:, 0:nb], ends[:, size - nb : size]], axis=1)
    for e in range(n):
        bits = [ports, field[:, e * per : (e + 1) * per]]
        if 2 * nb + per < 128:
            bits.append(jnp.zeros((2 * nb, 128 - 2 * nb - per), jnp.float32))
        msg_out[e] = jnp.concatenate(bits, axis=1)

    def msg_copy(off):
        peer = lax.rem(a + off, n)
        return pltpu.make_async_remote_copy(
            src_ref=msg_out.at[peer], dst_ref=msg_in.at[a], send_sem=s_msg.at[off], recv_sem=r_msg.at[off],
            device_id=(peer, c), device_id_type=MESH)

    def back_copy(off):
        peer = lax.rem(a + off, n)
        return pltpu.make_async_remote_copy(
            src_ref=back_out.at[peer], dst_ref=back_in.at[a], send_sem=s_back.at[off], recv_sem=r_back.at[off],
            device_id=(peer, c), device_id_type=MESH)

    for off in range(1, n):
        msg_copy(off).start()
    msg_in[a] = msg_out[a]

    half = rows * nz // 2
    for part in range(2):
        X[:, nz + part * half : nz + (part + 1) * half] = dot(G[...], F[:, nz + part * half : nz + (part + 1) * half])

    @pl.when(has_lo)
    def _():
        hal_copy(True).wait_send()
        hal_copy(False).wait_recv()

    @pl.when(has_hi)
    def _():
        hal_copy(False).wait_send()
        hal_copy(True).wait_recv()

    sides = dot(G[...], jnp.concatenate([F[:, 0:nz], F[:, (rows + 1) * nz : (rows + 2) * nz]], axis=1))
    X[:, 0:nz] = sides[:, 0:nz]
    X[:, (rows + 1) * nz : (rows + 2) * nz] = sides[:, nz : 2 * nz]

    for off in range(1, n):
        msg_copy(off).wait_recv()

    lane = lax.broadcasted_iota(jnp.int32, (1, 128), 1)
    keep_l = jnp.where((lane >= nb) & (lane < 2 * nb), 0.0, 1.0)
    keep_r = jnp.where(lane < nb, 0.0, 1.0)
    groups = [(msg_in[d][0:nb], msg_in[d][nb : 2 * nb], None) for d in range(n)]
    while len(groups) > 1:
        pairs = [(groups[i], groups[i + 1]) for i in range(0, len(groups), 2)]
        weights = invert([eye - dot(r[0][:, 0:nb], l[1][:, nb : 2 * nb]) for l, r in pairs])
        top = len(pairs) == 1
        groups = []
        for (l, r), w in zip(pairs, weights):
            from_l, from_r = l[1] * keep_l, r[0] * keep_r
            p = dot(w, from_r + dot(r[0][:, 0:nb], from_l))
            q = from_l + dot(l[1][:, nb : 2 * nb], p)
            left = l[0] if l[2] is None else jnp.concatenate([l[0], l[2]], axis=0)
            right = r[1] if r[2] is None else jnp.concatenate([r[1], r[2]], axis=0)
            left = left * keep_l + dot(left[:, nb : 2 * nb], p)
            right = right * keep_r + dot(right[:, 0:nb], q)
            inner = [p, q]
            if l[2] is not None:
                inner = [left[nb:]] + inner
            if r[2] is not None:
                inner = inner + [right[nb:]]
            groups.append((left[0:nb], right[0:nb], jnp.concatenate(inner, axis=0)))
    inner = groups[0][2]
    none = jnp.zeros((nb, 128), jnp.float32)
    for d in range(n):
        if d == 0:
            back_out[d] = jnp.concatenate([none, inner[0:nb]], axis=0)
        elif d == n - 1:
            back_out[d] = jnp.concatenate([inner[(2 * d - 1) * nb :], none], axis=0)
        else:
            back_out[d] = inner[(2 * d - 1) * nb : (2 * d + 1) * nb]
    for off in range(1, n):
        back_copy(off).start()
    back_in[a] = back_out[a]
    for off in range(1, n):
        back_copy(off).wait_recv()

    each = n // rows
    flux = []
    for y in range(rows):
        flux.append(jnp.concatenate([back_in[y * each + e][:, 2 * nb : 2 * nb + per] for e in range(each)], axis=1))
    edge_out[0] = flux[0]
    edge_out[1] = flux[rows - 1]

    @pl.when(has_lo)
    def _():
        edge_copy(True).start()

    @pl.when(has_hi)
    def _():
        edge_copy(False).start()

    gc = jnp.concatenate([G[:, 0:nb], G[:, size - nb : size]], axis=1)
    X[:, nz : (rows + 1) * nz] += dot(gc, jnp.concatenate(flux, axis=1))

    opens = []
    for y in range(-1, rows + 1):
        at = jnp.clip(c * rows + y, 0, nc * rows - 1)
        line = open_ref[pl.ds(at, 1), :].astype(jnp.float32)
        if y == -1:
            line = jnp.where(has_lo, line, 0.0)
        if y == rows:
            line = jnp.where(has_hi, line, 0.0)
        opens.append(line)

    segs = sum_out.shape[-1]
    seg_id = lax.broadcasted_iota(jnp.int32, (1, segs), 1)
    gain = jnp.zeros((8, segs), jnp.float32)
    for y in range(rows):
        bits = []
        for i in range(cells):
            sent = X[i * nb : (i + 1) * nb, (y + 1) * nz : (y + 2) * nz] * prof_col
            bits.append(jnp.sum(sent, axis=0, keepdims=True))
        given = jnp.sum(jnp.concatenate(bits, axis=0) * opens[y + 1], axis=1, keepdims=True) * (1.0 / nz)
        picked = jnp.where(seg_col[y] == seg_id.astype(jnp.float32), given, 0.0)
        for i in range(cells // 8):
            gain = gain + picked[i * 8 : (i + 1) * 8]
    sum_out[0] = gain

    def cross_copy(off):
        return pltpu.make_async_remote_copy(
            src_ref=sum_out.at[0], dst_ref=sum_cross.at[off], send_sem=s_cross.at[off], recv_sem=r_cross.at[off],
            device_id=(a, lax.rem(c + off, nc)), device_id_type=MESH)

    def axial_copy(off):
        return pltpu.make_async_remote_copy(
            src_ref=sum_out.at[1], dst_ref=sum_axial.at[off], send_sem=s_axial.at[off], recv_sem=r_axial.at[off],
            device_id=(lax.rem(a + off, n), c), device_id_type=MESH)

    for off in range(1, nc):
        cross_copy(off).start()

    @pl.when(has_lo)
    def _():
        edge_copy(True).wait_send()
        edge_copy(False).wait_recv()
        X[:, 0:nz] += dot(gc, edge_in[1])

    @pl.when(has_hi)
    def _():
        edge_copy(False).wait_send()
        edge_copy(True).wait_recv()
        X[:, (rows + 1) * nz : (rows + 2) * nz] += dot(gc, edge_in[0])

    zlane = lax.broadcasted_iota(jnp.int32, (1, nz), 1)
    step_col = jnp.concatenate([cross_col] * 4, axis=0)
    block = 4 * nb
    for y in range(rows):
        here = opens[y + 1]
        before = jnp.where(zlane == 0, 0.0, pltpu.roll(here, 1, 1)) * here
        after = jnp.where(zlane == nz - 1, 0.0, pltpu.roll(here, nz - 1, 1)) * here
        above = opens[y] * here
        below = opens[y + 2] * here
        total = before + after + above + below
        for i in range(size // block):
            at = slice(i * block, (i + 1) * block)
            x = X[at, (y + 1) * nz : (y + 2) * nz]
            moved = (above * (X[at, y * nz : (y + 1) * nz] - x) + below * (X[at, (y + 2) * nz : (y + 3) * nz] - x)
                     + before * (pltpu.roll(x, 1, 1) - x) + after * (pltpu.roll(x, nz - 1, 1) - x))
            out[pl.ds(i * block * rows + y, block, stride=rows), :] = x + step_col * moved
        if y == 0:
            gain = sum_out[0]
            for off in range(1, nc):
                cross_copy(off).wait_recv()
                gain = gain + sum_cross[off]
            sum_out[1] = gain
            for off in range(1, n):
                axial_copy(off).start()

    gain = sum_out[1]
    for off in range(1, n):
        axial_copy(off).wait_recv()
        gain = gain + sum_axial[off]
    gain = jnp.sum(gain, axis=0, keepdims=True)
    own = out_seg.shape[1]
    own_id = lax.broadcasted_iota(jnp.int32, (1, own), 1)
    result = jnp.zeros((1, own), jnp.float32)
    for j in range(own):
        mine = jnp.sum(jnp.where(seg_id == (a * nc + c) * own + j, gain, 0.0), axis=1, keepdims=True)
        result = jnp.where(own_id == j, mine, result)
    out_seg[...] = result

    for off in range(1, nc):
        cross_copy(off).wait_send()
    for off in range(1, n):
        axial_copy(off).wait_send()

    for off in range(1, n):
        msg_copy(off).wait_send()
        back_copy(off).wait_send()


def per_device(n, nc, cotangent, diag_blocks, lower_rates, upper_rates, cross_rate, bin_profile, open_cells, segment_ids):
    cells, nb, rows, nz = cotangent.shape
    size = cells * nb
    segs = SEG_DEV * n * nc
    vmem = pl.BlockSpec(memory_space=pltpu.VMEM)
    hbm = pl.BlockSpec(memory_space=pltpu.HBM)
    dma = pltpu.SemaphoreType.DMA
    f32 = jnp.float32
    operands = (
        cotangent.reshape(size * rows, nz), diag_blocks, lower_rates, upper_rates,
        cross_rate.reshape(1, nb), bin_profile.reshape(1, nb), open_cells, segment_ids.T,
    )
    grad, gain = pl.pallas_call(
        functools.partial(kernel, n, nc),
        out_shape=(jax.ShapeDtypeStruct((size * rows, nz), f32), jax.ShapeDtypeStruct((1, SEG_DEV), f32)),
        in_specs=[hbm] * len(operands),
        out_specs=(vmem, vmem),
        scratch_shapes=[pltpu.VMEM(x.shape, x.dtype) for x in operands] + [
            pltpu.VMEM((size, size), f32),
            pltpu.VMEM((size, (rows + 2) * nz), f32),
            pltpu.VMEM((size, (rows + 2) * nz), f32),
            pltpu.VMEM((128, 128), f32),
            pltpu.VMEM((n, 2 * nb, 128), f32),
            pltpu.VMEM((n, 2 * nb, 128), f32),
            pltpu.VMEM((n, 2 * nb, 128), f32),
            pltpu.VMEM((n, 2 * nb, 128), f32),
            pltpu.VMEM((2, 2 * nb, nz), f32),
            pltpu.VMEM((2, 2 * nb, nz), f32),
            pltpu.VMEM((2, 8, segs), f32),
            pltpu.VMEM((nc, 8, segs), f32),
            pltpu.VMEM((n, 8, segs), f32),
            dma((len(operands),)), dma((n,)), dma((n,)), dma((n,)), dma((n,)), dma((2,)), dma((2,)), dma((2,)), dma((2,)),
            dma((nc,)), dma((nc,)), dma((n,)), dma((n,)),
        ],
        compiler_params=pltpu.CompilerParams(
            collective_id=0, has_side_effects=True, vmem_limit_bytes=63 * 1024 * 1024 + 512 * 1024
        ),
    )(*operands)
    return grad.reshape(cotangent.shape), gain.reshape(SEG_DEV)


def solution(mesh):
    in_specs = (
        P("axial", None, "cross", None),
        P("axial", None, None),
        P("axial", None),
        P("axial", None),
        P(),
        P(),
        P(),
        P("axial", "cross"),
    )
    out_specs = (P("axial", None, "cross", None), P(("axial", "cross")))
    return jax.shard_map(
        functools.partial(per_device, mesh.shape["axial"], mesh.shape["cross"]),
        mesh=mesh, in_specs=in_specs, out_specs=out_specs, check_vma=False,
    )
```
